256 devices in a mesh: pair: 64 (over z, y, core), rep: 4 (over x).
Axes of the slice: x: 4, y: 4, z: 8, core: 2. Of those that a mesh axis runs over, the one named last changes fastest.
Arguments:
- t_amp: bfloat16 [65536, 1536], P('pair', 'rep'), may hold values from -6 to 6
- t_mask: int32 [512, 12], P('pair', 'rep'), may hold values 0 or 1
- v_int: bfloat16 [1536, 8192], P('rep', 'pair'), may hold values from -0.15625 to 0.15625
- v_mask: int32 [12, 64], P('rep', 'pair'), may hold values 0 or 1
- ab_order: int32 [64], replicated, may hold values from 0 to 63, each once
- r_mask: int32 [512, 64], P('pair', 'rep'), may hold values 0 or 1
- r_old: bfloat16 [65536, 8192], P('pair', 'rep'), may hold values from -6 to 6
Outputs:
- r_new: bfloat16 [65536, 8192], P('pair', 'rep')
The draws below stay inside these ranges and needn't reach their ends.
Inputs may be any that keep to these rules, and one draw needn't show every extreme that they name: `ab_order`: a permutation of the 64 tile indices.
All inputs are finite; a program needn't handle non-finite values. No bound on the sum of `t_mask` or of `v_mask` or of `r_mask` on one device may be relied on, other than what follows from the above.
Results may differ from the reference program's by a relative error of at most 0.001.
Values may be sent and summed in bfloat16 or wider, within the bound.
No kernel may reach another device: no remote copies, remote signals or barrier semaphores. Data moves between devices by JAX's collectives and lax.ppermute only.
A program may use at most 128 MiB of HBM per device.

```python
import jax
import jax.numpy as jnp
from jax import lax

TILE = 128
NI = 512
NC = 12
NA = 64


def set_ends(entries, stream_key, smallest, largest):
    longest = entries.shape.index(max(entries.shape))
    spots = []
    for shift in (0, 1):
        where = [jax.random.randint(jax.random.fold_in(stream_key, axis), (), 0, length) for axis, length in enumerate(entries.shape)]
        where[longest] = (where[longest] + shift) % entries.shape[longest]
        spots.append(tuple(where))
    return entries.at[spots[0]].set(smallest).at[spots[1]].set(largest)


def block_scale(key, extent, cuts, smallest, top_value):
    level, own = 1.0, jax.random.fold_in(key, 6)
    for axis_at, blocks in cuts:
        draws = jnp.exp(jax.random.uniform(jax.random.fold_in(own, axis_at), (blocks,), jnp.float32, smallest / len(cuts), top_value / len(cuts)))
        level = level * jnp.repeat(draws, extent[axis_at] // blocks).reshape([-1 if axis == axis_at else 1 for axis in range(len(extent))])
    return level


def scatter_about(key, extent, width, limit, cuts=(), kind=jnp.bfloat16):
    gain = block_scale(key, extent, cuts, -0.22, 0.18) if cuts else 1.0
    values = jax.random.normal(key, extent, jnp.float32) * width * gain
    return jnp.minimum(jnp.maximum(values, -limit), limit).astype(kind)


def setup_inputs(seed: int = 0) -> dict:
    arg_keys = jax.random.split(jax.random.key(seed), 8)
    return {
        "t_amp": scatter_about(arg_keys[0], (NI * TILE, NC * TILE), 1.0, 6.0, ((0, 64), (1, 4))),
        "t_mask": set_ends((jax.random.randint(arg_keys[1], (NI, NC), 0, 4) < 3).astype(jnp.int32), jax.random.fold_in(arg_keys[1], 1), 0, 1),
        "v_int": scatter_about(arg_keys[2], (NC * TILE, NA * TILE), (NC * TILE) ** -0.5, 0.15625, ((0, 4), (1, 64))),
        "v_mask": set_ends((jax.random.randint(arg_keys[3], (NC, NA), 0, 4) < 3).astype(jnp.int32), jax.random.fold_in(arg_keys[3], 1), 0, 1),
        "ab_order": jax.random.permutation(arg_keys[4], NA).astype(jnp.int32),
        "r_mask": set_ends((jax.random.randint(arg_keys[5], (NI, NA), 0, 4) < 3).astype(jnp.int32), jax.random.fold_in(arg_keys[5], 1), 0, 1),
        "r_old": scatter_about(arg_keys[6], (NI * TILE, NA * TILE), 1.0, 6.0, ((0, 64), (1, 4))),
    }


def reference(t_amp, t_mask, v_int, v_mask, ab_order, r_mask, r_old):
    t_kept = (t_amp.reshape(NI, TILE, NC, TILE) * t_mask[:, None, :, None].astype(t_amp.dtype)).reshape(NI * TILE, NC * TILE)
    v_kept = (v_int.reshape(NC, TILE, NA, TILE) * v_mask[:, None, :, None].astype(v_int.dtype)).reshape(NC * TILE, NA, TILE)
    inverse = jnp.zeros((NA,), jnp.int32).at[ab_order.astype(jnp.int32)].set(jnp.arange(NA, dtype=jnp.int32))
    v_natural = jnp.take(v_kept, inverse, axis=1).reshape(NC * TILE, NA * TILE)
    t_blocks = t_kept.reshape(NI, TILE, NC * TILE)
    r_blocks = r_old.reshape(NI, TILE, NA * TILE)

    def one_block(packed):
        t_rows, r_rows, m_rows = packed
        ladder = jnp.dot(t_rows, v_natural, preferred_element_type=jnp.float32).reshape(TILE, NA, TILE)
        kept = ladder * m_rows[None, :, None].astype(jnp.float32)
        return (r_rows.astype(jnp.float32) + kept.reshape(TILE, NA * TILE)).astype(jnp.bfloat16)

    result = lax.map(one_block, (t_blocks, r_blocks, r_mask))
    return result.reshape(NI * TILE, NA * TILE)
```

```python
import functools

import jax
import jax.numpy as jnp
from jax import lax
from jax.experimental import pallas as pl
from jax.experimental.pallas import tpu as pltpu
from jax.sharding import Mesh
from jax.sharding import PartitionSpec as P

TILE = 128
NZ, NY, NX = 8, 4, 4
CHUNK = 48
ROWS = 256
COLS = 16
SPAN = 8
BLOCKS = 16
HALF = 8
SMALL = 16 * 1024 * 1024
LARGE = 60 * 1024 * 1024


def pairs_zc(d):
    return [(z * 2 + c, ((z + (d if c == 0 else -d)) % NZ) * 2 + c) for z in range(NZ) for c in range(2)]


def pairs_yc(d):
    return [(y * 2 + c, ((y + (d if c == 0 else -d)) % NY) * 2 + c) for y in range(NY) for c in range(2)]


def pairs_cx(d):
    return [(c * NX + x, c * NX + (x + (d if c == 0 else -d)) % NX) for c in range(2) for x in range(NX)]


def move_z(v):
    return lax.ppermute(v, ("z", "c"), pairs_zc(1))


def move_y(v):
    return lax.ppermute(v, ("y", "c"), pairs_yc(1))


def move_x(v, d=1):
    return lax.ppermute(v, ("c", "x"), pairs_cx(d))


def swap(v):
    return lax.ppermute(v, "c", [(0, 1), (1, 0)])


def cost(flops, moved):
    return pl.CostEstimate(flops=flops, bytes_accessed=moved, transcendentals=0)


def in_smem():
    return pl.BlockSpec(memory_space=pltpu.SMEM)


def in_vmem():
    return pl.BlockSpec(memory_space=pltpu.VMEM)


def keep_t_kernel(mask_ref, t_ref, out_ref):
    i = pl.program_id(0)
    rows, cols = t_ref.shape
    for a in range(rows // TILE):
        for j in range(cols // TILE):
            at = (slice(a * TILE, (a + 1) * TILE), slice(j * TILE, (j + 1) * TILE))
            kept = mask_ref[i * (rows // TILE) + a, j] != 0
            out_ref[at] = jnp.where(kept, t_ref[at], jnp.zeros((TILE, TILE), t_ref.dtype))


def keep_t(mask, t):
    rows, cols = t.shape
    block = pl.BlockSpec((ROWS, cols), lambda i: (i, 0))
    return pl.pallas_call(
        keep_t_kernel,
        grid=(rows // ROWS,),
        out_shape=jax.ShapeDtypeStruct(t.shape, t.dtype),
        in_specs=[in_smem(), block],
        out_specs=block,
        compiler_params=pltpu.CompilerParams(vmem_limit_bytes=SMALL),
        cost_estimate=cost(rows * cols, 4 * rows * cols),
        name="keep_t",
    )(mask, t)


def spread_v_kernel(mask_ref, v_ref, out_ref):
    for g in range(8):
        for k in range(CHUNK // 16):
            row = g * CHUNK + k * 16
            kept = mask_ref[row // TILE, 0] != 0
            v = jnp.where(kept, v_ref[row : row + 16, :], jnp.zeros((16, TILE), v_ref.dtype))
            for zz in range(2):
                for yy in range(2):
                    chip = (zz * 4 + g // 2) * NY + yy * 2 + g % 2
                    out_ref[chip, k * 16 : k * 16 + 16, :] = v


def spread_v(mask, v):
    return pl.pallas_call(
        spread_v_kernel,
        out_shape=jax.ShapeDtypeStruct((NZ * NY, CHUNK, TILE), v.dtype),
        in_specs=[in_smem(), in_vmem()],
        out_specs=in_vmem(),
        compiler_params=pltpu.CompilerParams(vmem_limit_bytes=SMALL),
        cost_estimate=cost(v.size, 12 * v.size),
        name="spread_v",
    )(mask, v)


def select_kernel(place_ref, order_ref, a_ref, b_ref, own_ref, near_ref, far_ref, slot_ref):
    c, x = place_ref[2], place_ref[3]
    for k in range(order_ref.shape[0]):
        slot_ref[order_ref[k]] = k

    def put(out_ref, first, count):
        for j in range(count):
            k = slot_ref[first + j]
            chip = lax.div(k, 2)
            out_ref[j] = jnp.where(lax.rem(k, 2) == c, a_ref[chip], b_ref[chip])

    put(own_ref, x * COLS, COLS)
    put(near_ref, lax.rem(x + 1 - 2 * c + NX, NX) * COLS, COLS)
    put(far_ref, lax.rem(x + 2, NX) * COLS + c * HALF, HALF)


def select(place, order, a, b):
    shape = lambda n: jax.ShapeDtypeStruct((n, CHUNK, TILE), a.dtype)
    return pl.pallas_call(
        select_kernel,
        out_shape=(shape(COLS), shape(COLS), shape(HALF)),
        in_specs=[in_smem(), in_smem(), in_vmem(), in_vmem()],
        out_specs=(in_vmem(),) * 3,
        scratch_shapes=[pltpu.SMEM((order.shape[0],), jnp.int32)],
        compiler_params=pltpu.CompilerParams(vmem_limit_bytes=SMALL),
        cost_estimate=cost(0, 2 << 20),
        name="select_columns",
    )(place, order, a, b)


def pack_kernel(place_ref, own_ref, r1_ref, w1_ref, r2_ref, w2_ref, ahead_ref, rest_ref):
    c = place_ref[2]
    for j in range(COLS):
        opposite = jnp.where(c == j // HALF, r2_ref[j % HALF], w2_ref[j % HALF])
        left = jnp.where(c == 0, r1_ref[j], w1_ref[j])
        right = jnp.where(c == 0, w1_ref[j], r1_ref[j])
        ahead_ref[j, 0] = jnp.where(c == 0, own_ref[j], left)
        ahead_ref[j, 1] = jnp.where(c == 0, opposite, right)
        rest_ref[j, 0] = jnp.where(c == 0, left, own_ref[j])
        rest_ref[j, 1] = jnp.where(c == 0, right, opposite)


def pack(place, own, r1, w1, r2, w2):
    shape = jax.ShapeDtypeStruct((COLS, 2, CHUNK, TILE), own.dtype)
    return pl.pallas_call(
        pack_kernel,
        out_shape=(shape, shape),
        in_specs=[in_smem()] + [in_vmem()] * 5,
        out_specs=(in_vmem(),) * 2,
        compiler_params=pltpu.CompilerParams(vmem_limit_bytes=SMALL),
        cost_estimate=cost(0, 3 << 20),
        name="pack_shard",
    )(place, own, r1, w1, r2, w2)


def ladder_kernel(place_ref, mask_ref, t0, t1, t2, t3, r_ref, *rest):
    blocks, (out_ref, slab, sems) = rest[:BLOCKS], rest[BLOCKS:]
    i = pl.program_id(0)
    z, y, c = (place_ref[n] for n in range(3))
    s = 1 - 2 * c

    def copies(part):
        cols = pl.ds(part * SPAN, SPAN)
        zs = (z, z, z - s, z - s, z + s, z + s, z + 2, z + 2)
        halves = (c, 1 - c, c, 1 - c, 1 - c, c, c, 1 - c)
        for n, ref in enumerate(blocks):
            zz, half, yy = zs[n % 8], halves[n % 8], y + n // 8
            g = lax.rem(zz + NZ, 4) * 2 + lax.rem(yy, 2)
            yield pltpu.make_async_copy(ref.at[cols], slab.at[cols, pl.ds(2 * half, 2), g], sems.at[part, n])

    @pl.when(i == 0)
    def _():
        for part in range(COLS // SPAN):
            for copy in copies(part):
                copy.start()

    left = jnp.where(c == 0, t1[...], t2[...])
    right = jnp.where(c == 0, t2[...], t1[...])
    t = jnp.concatenate([t0[...], t3[...], left, right], axis=1)
    depth = t.shape[1]
    for n in range(COLS // 2):
        if 2 * n % SPAN == 0:

            @pl.when(i == 0)
            def _(part=2 * n // SPAN):
                for copy in copies(part):
                    copy.wait()

        pair = jnp.concatenate([slab[2 * n + k].reshape(depth, TILE) for k in range(2)], axis=1)
        acc = jnp.dot(t, pair, preferred_element_type=jnp.float32)
        for a in range(ROWS // TILE):
            rows = slice(a * TILE, (a + 1) * TILE)
            for j in range(2):
                cols = slice((2 * n + j) * TILE, (2 * n + j + 1) * TILE)
                m = mask_ref[i * (ROWS // TILE) + a, 2 * n + j].astype(jnp.float32)
                kept = acc[rows, j * TILE : (j + 1) * TILE] * m
                out_ref[rows, cols] = (r_ref[rows, cols].astype(jnp.float32) + kept).astype(out_ref.dtype)


def ladder(place, r_mask, ts, r_old, blocks):
    rows, width = r_old.shape
    part = ts[0].shape[1]
    depth = NX * part
    wide = pl.BlockSpec((ROWS, width), lambda i: (i, 0))
    return pl.pallas_call(
        ladder_kernel,
        grid=(rows // ROWS,),
        out_shape=jax.ShapeDtypeStruct(r_old.shape, r_old.dtype),
        in_specs=[in_smem(), in_smem()]
        + [pl.BlockSpec((ROWS, part), lambda i: (i, 0))] * NX
        + [wide]
        + [pl.BlockSpec(memory_space=pl.ANY)] * BLOCKS,
        out_specs=wide,
        scratch_shapes=[
            pltpu.VMEM((COLS, NX, 8, CHUNK, TILE), r_old.dtype),
            pltpu.SemaphoreType.DMA((COLS // SPAN, BLOCKS)),
        ],
        compiler_params=pltpu.CompilerParams(vmem_limit_bytes=LARGE, dimension_semantics=("arbitrary",)),
        cost_estimate=cost(2 * rows * depth * width, 4 * rows * width + 2 * rows * depth + 2 * depth * width),
        name="ladder",
    )(place, r_mask, *ts, r_old, *blocks)


def body(t_amp, t_mask, v_int, v_mask, ab_order, r_mask, r_old):
    z, y, c, x = (lax.axis_index(n) for n in ("z", "y", "c", "x"))
    place = jnp.stack([z, y, c, x]).astype(jnp.int32)

    t0 = keep_t(t_mask, t_amp)
    t1 = move_x(t0)
    t2 = move_x(t0, -1)
    t0, v_int = lax.optimization_barrier((t0, v_int))
    mine = lax.all_to_all(spread_v(v_mask, v_int), ("z", "y"), 0, 0)
    own, near, opposite = select(place, ab_order, mine, swap(mine))

    r1 = move_x(near)
    r2 = lax.ppermute(opposite, "x", [(i, (i + 2) % NX) for i in range(NX)])
    w1, w2 = swap(r1), swap(r2)
    ahead, rest = pack(place, own, r1, w1, r2, w2)
    t1, w2 = lax.optimization_barrier((t1, w2))
    t3 = move_x(t1)

    p1a, q0 = move_z(ahead), move_y(ahead)
    p1r = move_z(rest)
    p2, q1a = move_z(p1a), move_y(p1a)
    q1r, q2 = move_y(p1r), move_y(p2)
    blocks = [ahead, rest, p1a, p1r, swap(p1a), swap(p1r), p2, swap(p2)]
    blocks += [q0, swap(q0), q1a, q1r, swap(q1a), swap(q1r), q2, swap(q2)]
    return ladder(place, r_mask, (t0, t1, t2, t3), r_old, blocks)


def solution(mesh):
    torus = Mesh(mesh.devices.reshape(NZ, NY, 2, NX), ("z", "y", "c", "x"))
    pair = ("z", "y", "c")
    placed = (P(pair, "x"), P(pair, "x"), P("x", pair), P("x", pair), P(), P(pair, "x"), P(pair, "x"))
    return jax.shard_map(body, mesh=torus, in_specs=placed, out_specs=P(pair, "x"), check_vma=False)
```

```python
import functools

import jax
import jax.numpy as jnp
from jax import lax
from jax.experimental import pallas as pl
from jax.experimental.pallas import tpu as pltpu
from jax.sharding import Mesh
from jax.sharding import PartitionSpec as P

TILE = 128
NZ, NY, NX = 8, 4, 4
CHUNK = 48
ROWS = 256
COLS = 16
HALF = 8
SMALL = 16 * 1024 * 1024
LARGE = 28 * 1024 * 1024
WHOLE = 60 * 1024 * 1024


def pairs_zc(d):
    return [(z * 2 + c, ((z + (d if c == 0 else -d)) % NZ) * 2 + c) for z in range(NZ) for c in range(2)]


def pairs_yc(d):
    return [(y * 2 + c, ((y + (d if c == 0 else -d)) % NY) * 2 + c) for y in range(NY) for c in range(2)]


def pairs_cx(d):
    return [(c * NX + x, c * NX + (x + (d if c == 0 else -d)) % NX) for c in range(2) for x in range(NX)]


def move_z(name, v):
    with jax.named_scope(name):
        return lax.ppermute(v, ("z", "c"), pairs_zc(1))


def move_y(name, v):
    with jax.named_scope(name):
        return lax.ppermute(v, ("y", "c"), pairs_yc(1))


def move_x(name, v, d=1):
    with jax.named_scope(name):
        return lax.ppermute(v, ("c", "x"), pairs_cx(d))


def swap(name, v):
    with jax.named_scope(name):
        return lax.ppermute(v, "c", [(0, 1), (1, 0)])


def cost(flops, moved):
    return pl.CostEstimate(flops=flops, bytes_accessed=moved, transcendentals=0)


def in_smem():
    return pl.BlockSpec(memory_space=pltpu.SMEM)


def in_vmem():
    return pl.BlockSpec(memory_space=pltpu.VMEM)


def prepare_kernel(t_mask_ref, v_mask_ref, t_ref, v_ref, t_out, v_out, perm):
    rows, cols = t_ref.shape
    z, y, c = (lax.axis_index(n) for n in ("z", "y", "c"))
    s = 1 - 2 * c
    for g in range(8):
        for k in range(CHUNK // 16):
            row = g * CHUNK + k * 16
            v = v_ref[row : row + 16, :]
            v = jnp.where(v_mask_ref[0, row // TILE] != 0, v, jnp.zeros_like(v))
            for zz in range(2):
                for yy in range(2):
                    v_out[(zz * 4 + g // 2) * NY + yy * 2 + g % 2, k * 16 : k * 16 + 16, :] = v

    source = lax.broadcasted_iota(jnp.int32, (cols, cols), 0)
    target = lax.broadcasted_iota(jnp.int32, (cols, cols), 1)
    shift = jnp.zeros((1, cols), jnp.int32)
    lane = lax.broadcasted_iota(jnp.int32, (1, cols), 1)
    steps = ((0, 0), (-s, 0), (s, 0), (0, 1), (2, 0), (-s, 1), (s, 1), (2, 1))
    for q, (dz, dy) in enumerate(steps):
        g = lax.rem(z + dz + NZ, 4) * 2 + lax.rem(y + dy, 2)
        shift = jnp.where(lane >= q * CHUNK, (g - q) * CHUNK, shift)
    perm[...] = jnp.where(source == target + shift, 1.0, 0.0).astype(perm.dtype)

    @pl.loop(0, rows // TILE)
    def _(a):
        at = pl.ds(pl.multiple_of(a * TILE, TILE), TILE)
        tiles = []
        for j in range(cols // TILE):
            t = t_ref[at, j * TILE : (j + 1) * TILE]
            tiles.append(jnp.where(t_mask_ref[j, a] != 0, t, jnp.zeros_like(t)))
        kept = jnp.concatenate(tiles, axis=1)
        t_out[at, :] = jnp.dot(kept, perm[...], preferred_element_type=jnp.float32).astype(t_out.dtype)


def prepare(t_mask, v_mask, t, v):
    return pl.pallas_call(
        prepare_kernel,
        out_shape=(
            jax.ShapeDtypeStruct(t.shape, t.dtype),
            jax.ShapeDtypeStruct((NZ * NY, CHUNK, TILE), v.dtype),
        ),
        in_specs=[in_smem()] * 2 + [in_vmem()] * 2,
        out_specs=(in_vmem(), in_vmem()),
        scratch_shapes=[pltpu.VMEM((t.shape[1], t.shape[1]), t.dtype)],
        compiler_params=pltpu.CompilerParams(vmem_limit_bytes=WHOLE),
        cost_estimate=cost(2 * t.size * t.shape[1], 4 * t.size + 12 * v.size),
        name="prepare",
    )(t_mask.T, v_mask.T, t, v)


def select_kernel(pick_ref, a_ref, b_ref, own_ref, near_ref, far_ref):
    start = 0
    for out_ref in (own_ref, near_ref, far_ref):
        for j in range(out_ref.shape[0]):
            k = pick_ref[start + j]
            chip = lax.rem(k, NZ * NY)
            out_ref[j] = jnp.where(k < NZ * NY, a_ref[chip], b_ref[chip])
        start += out_ref.shape[0]


def select(picks, a, b):
    shape = lambda n: jax.ShapeDtypeStruct((n, CHUNK, TILE), a.dtype)
    return pl.pallas_call(
        select_kernel,
        out_shape=(shape(COLS), shape(COLS), shape(HALF)),
        in_specs=[in_smem(), in_vmem(), in_vmem()],
        out_specs=(in_vmem(),) * 3,
        compiler_params=pltpu.CompilerParams(vmem_limit_bytes=SMALL),
        cost_estimate=cost(0, 2 << 20),
        name="select_columns",
    )(picks, a, b)


def column_picks(order):
    c, x = lax.axis_index("c"), lax.axis_index("x")
    lane = jnp.arange(2 * COLS + HALF, dtype=jnp.int32)
    near = lax.rem(x + 1 - 2 * c + NX, NX) * COLS + lane - COLS
    far = lax.rem(x + 2, NX) * COLS + c * HALF + lane - 2 * COLS
    wanted = jnp.where(lane < COLS, x * COLS + lane, jnp.where(lane < 2 * COLS, near, far))
    stored = jnp.arange(order.shape[0], dtype=jnp.int32)
    held = stored // 2 + jnp.where(stored % 2 == c, 0, NZ * NY)
    return jnp.sum(jnp.where(order[None, :] == wanted[:, None], held[None, :], 0), axis=1).astype(jnp.int32)


def pack_kernel(own_ref, r1_ref, w1_ref, r2_ref, w2_ref, ahead_ref, rest_ref):
    c = lax.axis_index("c")
    for j in range(COLS):
        opposite = jnp.where(c == j // HALF, r2_ref[j % HALF], w2_ref[j % HALF])
        left = jnp.where(c == 0, r1_ref[j], w1_ref[j])
        right = jnp.where(c == 0, w1_ref[j], r1_ref[j])
        ahead_ref[j, 0] = jnp.where(c == 0, own_ref[j], left)
        ahead_ref[j, 1] = jnp.where(c == 0, opposite, right)
        rest_ref[j, 0] = jnp.where(c == 0, left, own_ref[j])
        rest_ref[j, 1] = jnp.where(c == 0, right, opposite)


def pack(own, r1, w1, r2, w2):
    shape = jax.ShapeDtypeStruct((COLS, 2, CHUNK, TILE), own.dtype)
    return pl.pallas_call(
        pack_kernel,
        out_shape=(shape, shape),
        in_specs=[in_vmem()] * 5,
        out_specs=(in_vmem(),) * 2,
        compiler_params=pltpu.CompilerParams(vmem_limit_bytes=SMALL),
        cost_estimate=cost(0, 3 << 20),
        name="pack_shard",
    )(own, r1, w1, r2, w2)


def arrange_kernel(t0, t1, t2, t3, early_ref, late_ref):
    c = lax.axis_index("c")
    rows, cols = t0.shape
    half = cols // 2

    def run(parts):
        @pl.loop(0, rows // TILE)
        def _(a):
            at = pl.ds(pl.multiple_of(a * TILE, TILE), TILE)
            whole = [p[at, :] for p in parts]
            early_ref[at, :] = jnp.concatenate([w[:, :half] for w in whole], axis=1)
            late_ref[at, :] = jnp.concatenate([w[:, half:] for w in whole], axis=1)

    @pl.when(c == 0)
    def _():
        run((t0, t3, t1, t2))

    @pl.when(c != 0)
    def _():
        run((t2, t1, t0, t3))


def arrange(ts):
    rows, cols = ts[0].shape
    shape = jax.ShapeDtypeStruct((rows, NX * cols // 2), ts[0].dtype)
    return pl.pallas_call(
        arrange_kernel,
        out_shape=(shape, shape),
        in_specs=[in_vmem()] * NX,
        out_specs=(in_vmem(), in_vmem()),
        compiler_params=pltpu.CompilerParams(vmem_limit_bytes=SMALL),
        cost_estimate=cost(0, 16 * rows * cols),
        name="arrange_t",
    )(*ts)


def product(t, blocks, n):
    columns = []
    for j in (n, n + 1):
        pieces = [blocks[q + r // 2 * 4][j, r % 2] for r in range(NX) for q in range(4)]
        columns.append(jnp.concatenate(pieces, axis=0))
    return jnp.dot(t, jnp.concatenate(columns, axis=1), preferred_element_type=jnp.float32)


def early_kernel(first, mask_ref, t_ref, r_ref, *rest):
    blocks, acc_ref = rest[:8], rest[8]

    @pl.loop(0, t_ref.shape[0] // ROWS)
    def _(i):
        at = pl.multiple_of(i * ROWS, ROWS)
        t = t_ref[pl.ds(at, ROWS), :]
        for n in range(0, HALF, 2):
            part = product(t, blocks, first + n)
            for a in range(ROWS // TILE):
                rows = pl.ds(pl.multiple_of(at + a * TILE, TILE), TILE)
                for j in range(2):
                    m = mask_ref[i * (ROWS // TILE) + a, first + n + j].astype(jnp.float32)
                    kept = part[a * TILE : (a + 1) * TILE, j * TILE : (j + 1) * TILE] * m
                    old = r_ref[rows, (first + n + j) * TILE : (first + n + j + 1) * TILE].astype(jnp.float32)
                    acc_ref[rows, (n + j) * TILE : (n + j + 1) * TILE] = old + kept


def early(first, r_mask, t, r_old, blocks):
    rows, depth = t.shape
    width = HALF * TILE
    return pl.pallas_call(
        functools.partial(early_kernel, first),
        out_shape=jax.ShapeDtypeStruct((rows, width), jnp.float32),
        in_specs=[in_smem()] + [in_vmem()] * 10,
        out_specs=in_vmem(),
        compiler_params=pltpu.CompilerParams(vmem_limit_bytes=LARGE),
        cost_estimate=cost(2 * rows * depth * width, 6 * rows * width + 2 * rows * depth + 2 * depth * width),
        name="ladder_early",
    )(r_mask, t, r_old, *blocks)


def late_kernel(mask_ref, t_ref, acc0, acc1, *rest):
    blocks, (out_ref, buffer, sems) = rest[:8], rest[8:]
    steps = t_ref.shape[0] // ROWS

    def send(i):
        rows = pl.ds(pl.multiple_of(i * ROWS, ROWS), ROWS)
        return pltpu.make_async_copy(buffer.at[i], out_ref.at[rows, :], sems.at[i])

    @pl.loop(0, steps)
    def _(i):
        at = pl.multiple_of(i * ROWS, ROWS)
        t = t_ref[pl.ds(at, ROWS), :]
        for n in range(0, COLS, 2):
            part = product(t, blocks, n)
            for a in range(ROWS // TILE):
                rows = pl.ds(pl.multiple_of(at + a * TILE, TILE), TILE)
                for j in range(2):
                    k = n + j
                    m = mask_ref[i * (ROWS // TILE) + a, k].astype(jnp.float32)
                    kept = part[a * TILE : (a + 1) * TILE, j * TILE : (j + 1) * TILE] * m
                    acc = (acc0, acc1)[k // HALF]
                    total = acc[rows, k % HALF * TILE : (k % HALF + 1) * TILE] + kept
                    buffer[i, a * TILE : (a + 1) * TILE, k * TILE : (k + 1) * TILE] = total.astype(buffer.dtype)
        send(i).start()

    @pl.loop(0, steps)
    def _(i):
        send(i).wait()


def late(r_mask, t, accs, blocks):
    rows, depth = t.shape
    width = COLS * TILE
    return pl.pallas_call(
        late_kernel,
        out_shape=jax.ShapeDtypeStruct((rows, width), t.dtype),
        in_specs=[in_smem()] + [in_vmem()] * 11,
        out_specs=pl.BlockSpec(memory_space=pl.ANY),
        scratch_shapes=[pltpu.VMEM((rows // ROWS, ROWS, width), t.dtype), pltpu.SemaphoreType.DMA((rows // ROWS,))],
        compiler_params=pltpu.CompilerParams(vmem_limit_bytes=LARGE),
        cost_estimate=cost(2 * rows * depth * width, 6 * rows * width + 2 * rows * depth + 2 * depth * width),
        name="ladder_late",
    )(r_mask, t, *accs, *blocks)


def body(t_amp, t_mask, v_int, v_mask, ab_order, r_mask, r_old):
    hold = lax.optimization_barrier
    picks = column_picks(ab_order)
    t0, spread = prepare(t_mask, v_mask, t_amp, v_int)
    t1 = move_x("t_near", t0)
    t2 = move_x("t_back", t0, -1)
    mine = lax.all_to_all(spread, ("z", "y"), 0, 0)
    partner = swap("v_swap", mine)
    own, near, opposite = select(picks, mine, partner)

    r1 = move_x("r_near", near)
    with jax.named_scope("r_far"):
        r2 = lax.ppermute(opposite, "x", [(i, (i + 2) % NX) for i in range(NX)])
    w1, w2 = swap("r_near_swap", r1), swap("r_far_swap", r2)
    t1, t2, w2 = hold((t1, t2, w2))
    ahead, rest = pack(own, r1, w1, r2, w2)
    t3 = move_x("t_far", t1)

    p1a = move_z("p1a", ahead)
    p1r = move_z("p1r", rest)
    q0 = move_y("q0", ahead)
    p2, q1a, q1r = move_z("p2", p1a), move_y("q1a", p1a), move_y("q1r", p1r)
    q2 = move_y("q2", p2)
    t_early, t_late = arrange((t0, t1, t2, t3))
    blocks = (ahead, p1a, swap("p1r_swap", p1r), q0, rest, p1r, swap("p1a_swap", p1a), swap("q0_swap", q0))
    acc0 = early(0, r_mask, t_early, r_old, blocks)
    p2, q1a, q1r, acc0 = hold((p2, q1a, q1r, acc0))
    acc1 = early(HALF, r_mask, t_early, r_old, blocks)
    q2, acc1 = hold((q2, acc1))
    swapped = [swap(n + "_swap", v) for n, v in (("q1r", q1r), ("p2", p2), ("q1a", q1a), ("q2", q2))]
    blocks = (p2, q1a, swapped[0], q2, swapped[1], q1r, swapped[2], swapped[3])
    return late(r_mask, t_late, (acc0, acc1), blocks)


def solution(mesh):
    torus = Mesh(mesh.devices.reshape(NZ, NY, 2, NX), ("z", "y", "c", "x"))
    pair = ("z", "y", "c")
    placed = (P(pair, "x"), P(pair, "x"), P("x", pair), P("x", pair), P(), P(pair, "x"), P(pair, "x"))
    return jax.shard_map(body, mesh=torus, in_specs=placed, out_specs=P(pair, "x"), check_vma=False)
```

```python
import functools

import jax
import jax.numpy as jnp
from jax import lax
from jax.experimental import pallas as pl
from jax.experimental.pallas import tpu as pltpu
from jax.sharding import Mesh
from jax.sharding import PartitionSpec as P

TILE = 128
NZ, NY, NX = 8, 4, 4
CHUNK = 48
ROWS = 256
COLS = 16
HALF = 8
SMALL = 16 * 1024 * 1024
LARGE = 28 * 1024 * 1024
WHOLE = 60 * 1024 * 1024


def pairs_zc(d):
    return [(z * 2 + c, ((z + (d if c == 0 else -d)) % NZ) * 2 + c) for z in range(NZ) for c in range(2)]


def pairs_yc(d):
    return [(y * 2 + c, ((y + (d if c == 0 else -d)) % NY) * 2 + c) for y in range(NY) for c in range(2)]


def pairs_cx(d):
    return [(c * NX + x, c * NX + (x + (d if c == 0 else -d)) % NX) for c in range(2) for x in range(NX)]


def move_z(name, v):
    with jax.named_scope(name):
        return lax.ppermute(v, ("z", "c"), pairs_zc(1))


def move_y(name, v):
    with jax.named_scope(name):
        return lax.ppermute(v, ("y", "c"), pairs_yc(1))


def move_x(name, v, d=1):
    with jax.named_scope(name):
        return lax.ppermute(v, ("c", "x"), pairs_cx(d))


def swap(name, v):
    with jax.named_scope(name):
        return lax.ppermute(v, "c", [(0, 1), (1, 0)])


def cost(flops, moved):
    return pl.CostEstimate(flops=flops, bytes_accessed=moved, transcendentals=0)


def in_smem():
    return pl.BlockSpec(memory_space=pltpu.SMEM)


def in_vmem():
    return pl.BlockSpec(memory_space=pltpu.VMEM)


def prepare_kernel(t_mask_ref, v_mask_ref, t_ref, v_ref, t_out, v_out, perm):
    rows, cols = t_ref.shape
    z, y, c = (lax.axis_index(n) for n in ("z", "y", "c"))
    s = 1 - 2 * c
    for g in range(8):
        for k in range(CHUNK // 16):
            row = g * CHUNK + k * 16
            v = v_ref[row : row + 16, :]
            v = jnp.where(v_mask_ref[0, row // TILE] != 0, v, jnp.zeros_like(v))
            for zz in range(2):
                for yy in range(2):
                    v_out[(zz * 4 + g // 2) * NY + yy * 2 + g % 2, k * 16 : k * 16 + 16, :] = v

    source = lax.broadcasted_iota(jnp.int32, (cols, cols), 0)
    target = lax.broadcasted_iota(jnp.int32, (cols, cols), 1)
    shift = jnp.zeros((1, cols), jnp.int32)
    lane = lax.broadcasted_iota(jnp.int32, (1, cols), 1)
    steps = ((0, 0), (-s, 0), (s, 0), (0, 1), (2, 0), (-s, 1), (s, 1), (2, 1))
    for q, (dz, dy) in enumerate(steps):
        g = lax.rem(z + dz + NZ, 4) * 2 + lax.rem(y + dy, 2)
        shift = jnp.where(lane >= q * CHUNK, (g - q) * CHUNK, shift)
    perm[...] = jnp.where(source == target + shift, 1.0, 0.0).astype(perm.dtype)

    @pl.loop(0, rows // TILE)
    def _(a):
        at = pl.ds(pl.multiple_of(a * TILE, TILE), TILE)
        tiles = []
        for j in range(cols // TILE):
            t = t_ref[at, j * TILE : (j + 1) * TILE]
            tiles.append(jnp.where(t_mask_ref[j, a] != 0, t, jnp.zeros_like(t)))
        kept = jnp.concatenate(tiles, axis=1)
        t_out[at, :] = jnp.dot(kept, perm[...], preferred_element_type=jnp.float32).astype(t_out.dtype)


def prepare(t_mask, v_mask, t, v):
    return pl.pallas_call(
        prepare_kernel,
        out_shape=(
            jax.ShapeDtypeStruct(t.shape, t.dtype),
            jax.ShapeDtypeStruct((NZ * NY, CHUNK, TILE), v.dtype),
        ),
        in_specs=[in_smem()] * 2 + [in_vmem()] * 2,
        out_specs=(in_vmem(), in_vmem()),
        scratch_shapes=[pltpu.VMEM((t.shape[1], t.shape[1]), t.dtype)],
        compiler_params=pltpu.CompilerParams(vmem_limit_bytes=WHOLE),
        cost_estimate=cost(2 * t.size * t.shape[1], 4 * t.size + 12 * v.size),
        name="prepare",
    )(t_mask.T, v_mask.T, t, v)


def select_kernel(pick_ref, a_ref, b_ref, own_ref, near_ref, far_ref):
    start = 0
    for out_ref in (own_ref, near_ref, far_ref):
        for j in range(out_ref.shape[0]):
            k = pick_ref[start + j]
            chip = lax.rem(k, NZ * NY)
            out_ref[j] = jnp.where(k < NZ * NY, a_ref[chip], b_ref[chip])
        start += out_ref.shape[0]


def select(picks, a, b):
    shape = lambda n: jax.ShapeDtypeStruct((n, CHUNK, TILE), a.dtype)
    return pl.pallas_call(
        select_kernel,
        out_shape=(shape(COLS), shape(COLS), shape(HALF)),
        in_specs=[in_smem(), in_vmem(), in_vmem()],
        out_specs=(in_vmem(),) * 3,
        compiler_params=pltpu.CompilerParams(vmem_limit_bytes=SMALL),
        cost_estimate=cost(0, 2 << 20),
        name="select_columns",
    )(picks, a, b)


def column_picks(order):
    c, x = lax.axis_index("c"), lax.axis_index("x")
    lane = jnp.arange(2 * COLS + HALF, dtype=jnp.int32)
    near = lax.rem(x + 1 - 2 * c + NX, NX) * COLS + lane - COLS
    far = lax.rem(x + 2, NX) * COLS + c * HALF + lane - 2 * COLS
    wanted = jnp.where(lane < COLS, x * COLS + lane, jnp.where(lane < 2 * COLS, near, far))
    stored = jnp.arange(order.shape[0], dtype=jnp.int32)
    held = stored // 2 + jnp.where(stored % 2 == c, 0, NZ * NY)
    return jnp.sum(jnp.where(order[None, :] == wanted[:, None], held[None, :], 0), axis=1).astype(jnp.int32)


def pack_kernel(own_ref, r1_ref, w1_ref, r2_ref, w2_ref, ahead_ref, rest_ref):
    c = lax.axis_index("c")
    for j in range(COLS):
        opposite = jnp.where(c == j // HALF, r2_ref[j % HALF], w2_ref[j % HALF])
        left = jnp.where(c == 0, r1_ref[j], w1_ref[j])
        right = jnp.where(c == 0, w1_ref[j], r1_ref[j])
        ahead_ref[j, 0] = jnp.where(c == 0, own_ref[j], left)
        ahead_ref[j, 1] = jnp.where(c == 0, opposite, right)
        rest_ref[j, 0] = jnp.where(c == 0, left, own_ref[j])
        rest_ref[j, 1] = jnp.where(c == 0, right, opposite)


def pack(own, r1, w1, r2, w2):
    shape = jax.ShapeDtypeStruct((COLS, 2, CHUNK, TILE), own.dtype)
    return pl.pallas_call(
        pack_kernel,
        out_shape=(shape, shape),
        in_specs=[in_vmem()] * 5,
        out_specs=(in_vmem(),) * 2,
        compiler_params=pltpu.CompilerParams(vmem_limit_bytes=SMALL),
        cost_estimate=cost(0, 3 << 20),
        name="pack_shard",
    )(own, r1, w1, r2, w2)


def arrange_kernel(t0, t1, t2, t3, early_ref, late_ref):
    c = lax.axis_index("c")
    rows, cols = t0.shape
    half = cols // 2

    def run(parts):
        @pl.loop(0, rows // TILE)
        def _(a):
            at = pl.ds(pl.multiple_of(a * TILE, TILE), TILE)
            whole = [p[at, :] for p in parts]
            early_ref[at, :] = jnp.concatenate([w[:, :half] for w in whole], axis=1)
            late_ref[at, :] = jnp.concatenate([w[:, half:] for w in whole], axis=1)

    @pl.when(c == 0)
    def _():
        run((t0, t3, t1, t2))

    @pl.when(c != 0)
    def _():
        run((t2, t1, t0, t3))


def arrange(ts):
    rows, cols = ts[0].shape
    shape = jax.ShapeDtypeStruct((rows, NX * cols // 2), ts[0].dtype)
    return pl.pallas_call(
        arrange_kernel,
        out_shape=(shape, shape),
        in_specs=[in_vmem()] * NX,
        out_specs=(in_vmem(), in_vmem()),
        compiler_params=pltpu.CompilerParams(vmem_limit_bytes=SMALL),
        cost_estimate=cost(0, 16 * rows * cols),
        name="arrange_t",
    )(*ts)


def product(t, blocks, n):
    columns = []
    for j in (n, n + 1):
        pieces = [blocks[q + r // 2 * 4][j, r % 2] for r in range(NX) for q in range(4)]
        columns.append(jnp.concatenate(pieces, axis=0))
    return jnp.dot(t, jnp.concatenate(columns, axis=1), preferred_element_type=jnp.float32)


def early_kernel(first, mask_ref, t_ref, r_ref, *rest):
    blocks, acc_ref = rest[:8], rest[8]

    @pl.loop(0, t_ref.shape[0] // ROWS)
    def _(i):
        at = pl.multiple_of(i * ROWS, ROWS)
        t = t_ref[pl.ds(at, ROWS), :]
        for n in range(0, HALF, 2):
            part = product(t, blocks, first + n)
            for a in range(ROWS // TILE):
                rows = pl.ds(pl.multiple_of(at + a * TILE, TILE), TILE)
                for j in range(2):
                    m = mask_ref[i * (ROWS // TILE) + a, first + n + j].astype(jnp.float32)
                    kept = part[a * TILE : (a + 1) * TILE, j * TILE : (j + 1) * TILE] * m
                    old = r_ref[rows, (first + n + j) * TILE : (first + n + j + 1) * TILE].astype(jnp.float32)
                    acc_ref[rows, (n + j) * TILE : (n + j + 1) * TILE] = old + kept


def early(first, r_mask, t, r_old, blocks):
    rows, depth = t.shape
    width = HALF * TILE
    return pl.pallas_call(
        functools.partial(early_kernel, first),
        out_shape=jax.ShapeDtypeStruct((rows, width), jnp.float32),
        in_specs=[in_smem()] + [in_vmem()] * 10,
        out_specs=in_vmem(),
        compiler_params=pltpu.CompilerParams(vmem_limit_bytes=LARGE),
        cost_estimate=cost(2 * rows * depth * width, 6 * rows * width + 2 * rows * depth + 2 * depth * width),
        name="ladder_early",
    )(r_mask, t, r_old, *blocks)


def late_kernel(mask_ref, t_ref, acc0, acc1, *rest):
    blocks, (out_ref, buffer, sems) = rest[:8], rest[8:]
    steps = t_ref.shape[0] // ROWS

    def send(i):
        rows = pl.ds(pl.multiple_of(i * ROWS, ROWS), ROWS)
        return pltpu.make_async_copy(buffer.at[i], out_ref.at[rows, :], sems.at[i])

    @pl.loop(0, steps)
    def _(i):
        at = pl.multiple_of(i * ROWS, ROWS)
        t = t_ref[pl.ds(at, ROWS), :]
        for n in range(0, COLS, 2):
            part = product(t, blocks, n)
            for a in range(ROWS // TILE):
                rows = pl.ds(pl.multiple_of(at + a * TILE, TILE), TILE)
                for j in range(2):
                    k = n + j
                    m = mask_ref[i * (ROWS // TILE) + a, k].astype(jnp.float32)
                    kept = part[a * TILE : (a + 1) * TILE, j * TILE : (j + 1) * TILE] * m
                    acc = (acc0, acc1)[k // HALF]
                    total = acc[rows, k % HALF * TILE : (k % HALF + 1) * TILE] + kept
                    buffer[i, a * TILE : (a + 1) * TILE, k * TILE : (k + 1) * TILE] = total.astype(buffer.dtype)
        send(i).start()

    @pl.loop(0, steps)
    def _(i):
        send(i).wait()


def late(r_mask, t, accs, blocks):
    rows, depth = t.shape
    width = COLS * TILE
    return pl.pallas_call(
        late_kernel,
        out_shape=jax.ShapeDtypeStruct((rows, width), t.dtype),
        in_specs=[in_smem()] + [in_vmem()] * 11,
        out_specs=pl.BlockSpec(memory_space=pl.ANY),
        scratch_shapes=[pltpu.VMEM((rows // ROWS, ROWS, width), t.dtype), pltpu.SemaphoreType.DMA((rows // ROWS,))],
        compiler_params=pltpu.CompilerParams(vmem_limit_bytes=LARGE),
        cost_estimate=cost(2 * rows * depth * width, 6 * rows * width + 2 * rows * depth + 2 * depth * width),
        name="ladder_late",
    )(r_mask, t, *accs, *blocks)


def body(t_amp, t_mask, v_int, v_mask, ab_order, r_mask, r_old):
    hold = lax.optimization_barrier
    picks = column_picks(ab_order)
    t0, spread = prepare(t_mask, v_mask, t_amp, v_int)
    t1 = move_x("t_near", t0)
    t2 = move_x("t_back", t0, -1)
    mine = lax.all_to_all(spread, ("z", "y"), 0, 0)
    partner = swap("v_swap", mine)
    own, near, opposite = select(picks, mine, partner)

    r1 = move_x("r_near", near)
    with jax.named_scope("r_far"):
        r2 = lax.ppermute(opposite, "x", [(i, (i + 2) % NX) for i in range(NX)])
    t1, t2, r1 = hold((t1, t2, r1))
    t3 = move_x("t_far", t1)
    w1, w2 = swap("r_near_swap", r1), swap("r_far_swap", r2)
    ahead, rest = pack(own, r1, w1, r2, w2)

    p1a = move_z("p1a", ahead)
    p1r = move_z("p1r", rest)
    q0 = move_y("q0", ahead)
    p2, q1a, q1r = move_z("p2", p1a), move_z("q1a", q0), move_y("q1r", p1r)
    q2 = move_y("q2", p2)
    t_early, t_late = arrange((t0, t1, t2, t3))
    p1a_swap, near_r, t_early = hold((swap("p1a_swap", p1a), p1r, t_early))
    p1r_swap = swap("p1r_swap", near_r)
    blocks = (ahead, p1a, p1r_swap, q0, rest, p1r, p1a_swap, swap("q0_swap", q0))
    acc0 = early(0, r_mask, t_early, r_old, blocks)
    p2, q1a, q1r, acc0 = hold((p2, q1a, q1r, acc0))
    acc1 = early(HALF, r_mask, t_early, r_old, blocks)
    q2, acc1 = hold((q2, acc1))
    swapped = [swap(n + "_swap", v) for n, v in (("q1r", q1r), ("p2", p2), ("q1a", q1a), ("q2", q2))]
    blocks = (p2, q1a, swapped[0], q2, swapped[1], q1r, swapped[2], swapped[3])
    return late(r_mask, t_late, (acc0, acc1), blocks)


def solution(mesh):
    torus = Mesh(mesh.devices.reshape(NZ, NY, 2, NX), ("z", "y", "c", "x"))
    pair = ("z", "y", "c")
    placed = (P(pair, "x"), P(pair, "x"), P("x", pair), P("x", pair), P(), P(pair, "x"), P(pair, "x"))
    return jax.shard_map(body, mesh=torus, in_specs=placed, out_specs=P(pair, "x"), check_vma=False)
```

```python
import functools

import jax
import jax.numpy as jnp
from jax import lax
from jax.experimental import pallas as pl
from jax.experimental.pallas import tpu as pltpu
from jax.sharding import Mesh
from jax.sharding import PartitionSpec as P

TILE = 128
NZ, NY, NX = 8, 4, 4
CHUNK = 48
ROWS = 256
COLS = 16
HALF = 8
SMALL = 16 * 1024 * 1024
LARGE = 28 * 1024 * 1024
WHOLE = 60 * 1024 * 1024


def pairs_zc(d):
    return [(z * 2 + c, ((z + (d if c == 0 else -d)) % NZ) * 2 + c) for z in range(NZ) for c in range(2)]


def pairs_yc(d):
    return [(y * 2 + c, ((y + (d if c == 0 else -d)) % NY) * 2 + c) for y in range(NY) for c in range(2)]


def pairs_cx(d):
    return [(c * NX + x, c * NX + (x + (d if c == 0 else -d)) % NX) for c in range(2) for x in range(NX)]


def move_z(name, v):
    with jax.named_scope(name):
        return lax.ppermute(v, ("z", "c"), pairs_zc(1))


def move_y(name, v):
    with jax.named_scope(name):
        return lax.ppermute(v, ("y", "c"), pairs_yc(1))


def move_x(name, v, d=1):
    with jax.named_scope(name):
        return lax.ppermute(v, ("c", "x"), pairs_cx(d))


def swap(name, v):
    with jax.named_scope(name):
        return lax.ppermute(v, "c", [(0, 1), (1, 0)])


def cost(flops, moved):
    return pl.CostEstimate(flops=flops, bytes_accessed=moved, transcendentals=0)


def in_smem():
    return pl.BlockSpec(memory_space=pltpu.SMEM)


def in_vmem():
    return pl.BlockSpec(memory_space=pltpu.VMEM)


def prepare_kernel(t_mask_ref, v_mask_ref, t_ref, v_ref, t_out, v_out, perm):
    rows, cols = t_ref.shape
    z, y, c = (lax.axis_index(n) for n in ("z", "y", "c"))
    s = 1 - 2 * c
    for g in range(8):
        for k in range(CHUNK // 16):
            row = g * CHUNK + k * 16
            v = v_ref[row : row + 16, :]
            v = jnp.where(v_mask_ref[0, row // TILE] != 0, v, jnp.zeros_like(v))
            for zz in range(2):
                for yy in range(2):
                    v_out[(zz * 4 + g // 2) * NY + yy * 2 + g % 2, k * 16 : k * 16 + 16, :] = v

    source = lax.broadcasted_iota(jnp.int32, (cols, cols), 0)
    target = lax.broadcasted_iota(jnp.int32, (cols, cols), 1)
    shift = jnp.zeros((1, cols), jnp.int32)
    lane = lax.broadcasted_iota(jnp.int32, (1, cols), 1)
    steps = ((0, 0), (-s, 0), (s, 0), (0, 1), (2, 0), (-s, 1), (s, 1), (2, 1))
    for q, (dz, dy) in enumerate(steps):
        g = lax.rem(z + dz + NZ, 4) * 2 + lax.rem(y + dy, 2)
        shift = jnp.where(lane >= q * CHUNK, (g - q) * CHUNK, shift)
    perm[...] = jnp.where(source == target + shift, 1.0, 0.0).astype(perm.dtype)

    @pl.loop(0, rows // ROWS)
    def _(i):
        start = pl.multiple_of(i * ROWS, ROWS)
        bands = []
        for a in range(ROWS // TILE):
            tiles = []
            for j in range(cols // TILE):
                t = t_ref[pl.ds(start + a * TILE, TILE), j * TILE : (j + 1) * TILE]
                tiles.append(jnp.where(t_mask_ref[j, i * (ROWS // TILE) + a] != 0, t, jnp.zeros_like(t)))
            bands.append(jnp.concatenate(tiles, axis=1))
        kept = jnp.concatenate(bands, axis=0)
        t_out[pl.ds(start, ROWS), :] = jnp.dot(kept, perm[...], preferred_element_type=jnp.float32).astype(t_out.dtype)


def prepare(t_mask, v_mask, t, v):
    return pl.pallas_call(
        prepare_kernel,
        out_shape=(
            jax.ShapeDtypeStruct(t.shape, t.dtype),
            jax.ShapeDtypeStruct((NZ * NY, CHUNK, TILE), v.dtype),
        ),
        in_specs=[in_smem()] * 2 + [in_vmem()] * 2,
        out_specs=(in_vmem(), in_vmem()),
        scratch_shapes=[pltpu.VMEM((t.shape[1], t.shape[1]), t.dtype)],
        compiler_params=pltpu.CompilerParams(vmem_limit_bytes=WHOLE),
        cost_estimate=cost(2 * t.size * t.shape[1], 4 * t.size + 12 * v.size),
        name="prepare",
    )(t_mask.T, v_mask.T, t, v)


def select_kernel(pick_ref, a_ref, b_ref, own_ref, near_ref, far_ref):
    start = 0
    for out_ref in (own_ref, near_ref, far_ref):
        for j in range(out_ref.shape[0]):
            k = pick_ref[start + j]
            chip = lax.rem(k, NZ * NY)
            out_ref[j] = jnp.where(k < NZ * NY, a_ref[chip], b_ref[chip])
        start += out_ref.shape[0]


def select(picks, a, b):
    shape = lambda n: jax.ShapeDtypeStruct((n, CHUNK, TILE), a.dtype)
    return pl.pallas_call(
        select_kernel,
        out_shape=(shape(COLS), shape(COLS), shape(HALF)),
        in_specs=[in_smem(), in_vmem(), in_vmem()],
        out_specs=(in_vmem(),) * 3,
        compiler_params=pltpu.CompilerParams(vmem_limit_bytes=SMALL),
        cost_estimate=cost(0, 2 << 20),
        name="select_columns",
    )(picks, a, b)


def column_picks(order):
    c, x = lax.axis_index("c"), lax.axis_index("x")
    lane = jnp.arange(2 * COLS + HALF, dtype=jnp.int32)
    near = lax.rem(x + 1 - 2 * c + NX, NX) * COLS + lane - COLS
    far = lax.rem(x + 2, NX) * COLS + c * HALF + lane - 2 * COLS
    wanted = jnp.where(lane < COLS, x * COLS + lane, jnp.where(lane < 2 * COLS, near, far))
    stored = jnp.arange(order.shape[0], dtype=jnp.int32)
    held = stored // 2 + jnp.where(stored % 2 == c, 0, NZ * NY)
    return jnp.sum(jnp.where(order[None, :] == wanted[:, None], held[None, :], 0), axis=1).astype(jnp.int32)


def pack_kernel(own_ref, r1_ref, w1_ref, r2_ref, w2_ref, ahead_ref, rest_ref):
    c = lax.axis_index("c")
    for j in range(COLS):
        opposite = jnp.where(c == j // HALF, r2_ref[j % HALF], w2_ref[j % HALF])
        left = jnp.where(c == 0, r1_ref[j], w1_ref[j])
        right = jnp.where(c == 0, w1_ref[j], r1_ref[j])
        ahead_ref[j, 0] = jnp.where(c == 0, own_ref[j], left)
        ahead_ref[j, 1] = jnp.where(c == 0, opposite, right)
        rest_ref[j, 0] = jnp.where(c == 0, left, own_ref[j])
        rest_ref[j, 1] = jnp.where(c == 0, right, opposite)


def pack(own, r1, w1, r2, w2):
    shape = jax.ShapeDtypeStruct((COLS, 2, CHUNK, TILE), own.dtype)
    return pl.pallas_call(
        pack_kernel,
        out_shape=(shape, shape),
        in_specs=[in_vmem()] * 5,
        out_specs=(in_vmem(),) * 2,
        compiler_params=pltpu.CompilerParams(vmem_limit_bytes=SMALL),
        cost_estimate=cost(0, 3 << 20),
        name="pack_shard",
    )(own, r1, w1, r2, w2)


def arrange_kernel(t0, t1, t2, t3, early_ref, late_ref):
    c = lax.axis_index("c")
    rows, cols = t0.shape
    half = cols // 2

    def run(parts):
        @pl.loop(0, rows // TILE)
        def _(a):
            at = pl.ds(pl.multiple_of(a * TILE, TILE), TILE)
            whole = [p[at, :] for p in parts]
            early_ref[at, :] = jnp.concatenate([w[:, :half] for w in whole], axis=1)
            late_ref[at, :] = jnp.concatenate([w[:, half:] for w in whole], axis=1)

    @pl.when(c == 0)
    def _():
        run((t0, t3, t1, t2))

    @pl.when(c != 0)
    def _():
        run((t2, t1, t0, t3))


def arrange(ts):
    rows, cols = ts[0].shape
    shape = jax.ShapeDtypeStruct((rows, NX * cols // 2), ts[0].dtype)
    return pl.pallas_call(
        arrange_kernel,
        out_shape=(shape, shape),
        in_specs=[in_vmem()] * NX,
        out_specs=(in_vmem(), in_vmem()),
        compiler_params=pltpu.CompilerParams(vmem_limit_bytes=SMALL),
        cost_estimate=cost(0, 16 * rows * cols),
        name="arrange_t",
    )(*ts)


def product(t, blocks, n):
    columns = []
    for j in (n, n + 1):
        pieces = [blocks[q + r // 2 * 4][j, r % 2] for r in range(NX) for q in range(4)]
        columns.append(jnp.concatenate(pieces, axis=0))
    return jnp.dot(t, jnp.concatenate(columns, axis=1), preferred_element_type=jnp.float32)


def early_kernel(first, mask_ref, t_ref, r_ref, *rest):
    blocks, acc_ref = rest[:8], rest[8]

    @pl.loop(0, t_ref.shape[0] // ROWS)
    def _(i):
        at = pl.multiple_of(i * ROWS, ROWS)
        t = t_ref[pl.ds(at, ROWS), :]
        for n in range(0, HALF, 2):
            part = product(t, blocks, first + n)
            for a in range(ROWS // TILE):
                rows = pl.ds(pl.multiple_of(at + a * TILE, TILE), TILE)
                for j in range(2):
                    m = mask_ref[i * (ROWS // TILE) + a, first + n + j].astype(jnp.float32)
                    kept = part[a * TILE : (a + 1) * TILE, j * TILE : (j + 1) * TILE] * m
                    old = r_ref[rows, (first + n + j) * TILE : (first + n + j + 1) * TILE].astype(jnp.float32)
                    acc_ref[rows, (n + j) * TILE : (n + j + 1) * TILE] = old + kept


def early(first, r_mask, t, r_old, blocks):
    rows, depth = t.shape
    width = HALF * TILE
    return pl.pallas_call(
        functools.partial(early_kernel, first),
        out_shape=jax.ShapeDtypeStruct((rows, width), jnp.float32),
        in_specs=[in_smem()] + [in_vmem()] * 10,
        out_specs=in_vmem(),
        compiler_params=pltpu.CompilerParams(vmem_limit_bytes=LARGE),
        cost_estimate=cost(2 * rows * depth * width, 6 * rows * width + 2 * rows * depth + 2 * depth * width),
        name="ladder_early",
    )(r_mask, t, r_old, *blocks)


def late_kernel(mask_ref, t_ref, acc0, acc1, *rest):
    blocks, (out_ref, buffer, sems) = rest[:8], rest[8:]
    steps = t_ref.shape[0] // ROWS

    def send(i):
        rows = pl.ds(pl.multiple_of(i * ROWS, ROWS), ROWS)
        return pltpu.make_async_copy(buffer.at[i], out_ref.at[rows, :], sems.at[i])

    @pl.loop(0, steps)
    def _(i):
        at = pl.multiple_of(i * ROWS, ROWS)
        t = t_ref[pl.ds(at, ROWS), :]
        for n in range(0, COLS, 2):
            part = product(t, blocks, n)
            for a in range(ROWS // TILE):
                rows = pl.ds(pl.multiple_of(at + a * TILE, TILE), TILE)
                for j in range(2):
                    k = n + j
                    m = mask_ref[i * (ROWS // TILE) + a, k].astype(jnp.float32)
                    kept = part[a * TILE : (a + 1) * TILE, j * TILE : (j + 1) * TILE] * m
                    acc = (acc0, acc1)[k // HALF]
                    total = acc[rows, k % HALF * TILE : (k % HALF + 1) * TILE] + kept
                    buffer[i, a * TILE : (a + 1) * TILE, k * TILE : (k + 1) * TILE] = total.astype(buffer.dtype)
        send(i).start()

    @pl.loop(0, steps)
    def _(i):
        send(i).wait()


def late(r_mask, t, accs, blocks):
    rows, depth = t.shape
    width = COLS * TILE
    return pl.pallas_call(
        late_kernel,
        out_shape=jax.ShapeDtypeStruct((rows, width), t.dtype),
        in_specs=[in_smem()] + [in_vmem()] * 11,
        out_specs=pl.BlockSpec(memory_space=pl.ANY),
        scratch_shapes=[pltpu.VMEM((rows // ROWS, ROWS, width), t.dtype), pltpu.SemaphoreType.DMA((rows // ROWS,))],
        compiler_params=pltpu.CompilerParams(vmem_limit_bytes=LARGE),
        cost_estimate=cost(2 * rows * depth * width, 6 * rows * width + 2 * rows * depth + 2 * depth * width),
        name="ladder_late",
    )(r_mask, t, *accs, *blocks)


def body(t_amp, t_mask, v_int, v_mask, ab_order, r_mask, r_old):
    hold = lax.optimization_barrier
    picks = column_picks(ab_order)
    t0, spread = prepare(t_mask, v_mask, t_amp, v_int)
    t1 = move_x("t_near", t0)
    t2 = move_x("t_back", t0, -1)
    mine = lax.all_to_all(spread, ("z", "y"), 0, 0)
    partner = swap("v_swap", mine)
    own, near, opposite = select(picks, mine, partner)

    r1 = move_x("r_near", near)
    with jax.named_scope("r_far"):
        r2 = lax.ppermute(opposite, "x", [(i, (i + 2) % NX) for i in range(NX)])
    t1, t2, r1 = hold((t1, t2, r1))
    t3 = move_x("t_far", t1)
    w1, w2 = swap("r_near_swap", r1), swap("r_far_swap", r2)
    ahead, rest = pack(own, r1, w1, r2, w2)

    p1a = move_z("p1a", ahead)
    p1r = move_z("p1r", rest)
    q0 = move_y("q0", ahead)
    p2, q1a, q1r = move_z("p2", p1a), move_z("q1a", q0), move_y("q1r", p1r)
    q2 = move_y("q2", p2)
    t_early, t_late = arrange((t0, t1, t2, t3))
    p1a_swap, near_r, t_early = hold((swap("p1a_swap", p1a), p1r, t_early))
    p1r_swap = swap("p1r_swap", near_r)
    blocks = (ahead, p1a, p1r_swap, q0, rest, p1r, p1a_swap, swap("q0_swap", q0))
    acc0 = early(0, r_mask, t_early, r_old, blocks)
    p2h, acc0 = hold((p2, acc0))
    acc1 = early(HALF, r_mask, t_early, r_old, blocks)
    q1a, q1r, acc1 = hold((q1a, q1r, acc1))
    q1a_swap, q1r_swap, p2_swap = swap("q1a_swap", q1a), swap("q1r_swap", q1r), swap("p2_swap", p2h)
    q2, q1a_swap, q1r_swap, p2_swap = hold((q2, q1a_swap, q1r_swap, p2_swap))
    accs = (acc0, acc1)
    blocks = (p2h, q1a, q1r_swap, q2, p2_swap, q1r, q1a_swap, swap("q2_swap", q2))
    return late(r_mask, t_late, accs, blocks)


def solution(mesh):
    torus = Mesh(mesh.devices.reshape(NZ, NY, 2, NX), ("z", "y", "c", "x"))
    pair = ("z", "y", "c")
    placed = (P(pair, "x"), P(pair, "x"), P("x", pair), P("x", pair), P(), P(pair, "x"), P(pair, "x"))
    return jax.shard_map(body, mesh=torus, in_specs=placed, out_specs=P(pair, "x"), check_vma=False)
```

```python
import functools

import jax
import jax.numpy as jnp
from jax import lax
from jax.experimental import pallas as pl
from jax.experimental.pallas import tpu as pltpu
from jax.sharding import Mesh
from jax.sharding import PartitionSpec as P

TILE = 128
NZ, NY, NX = 8, 4, 4
CHUNK = 48
ROWS = 256
COLS = 16
HALF = 8
SMALL = 16 * 1024 * 1024
LARGE = 28 * 1024 * 1024
WHOLE = 60 * 1024 * 1024


def pairs_zc(d):
    return [(z * 2 + c, ((z + (d if c == 0 else -d)) % NZ) * 2 + c) for z in range(NZ) for c in range(2)]


def pairs_yc(d):
    return [(y * 2 + c, ((y + (d if c == 0 else -d)) % NY) * 2 + c) for y in range(NY) for c in range(2)]


def pairs_cx(d):
    return [(c * NX + x, c * NX + (x + (d if c == 0 else -d)) % NX) for c in range(2) for x in range(NX)]


def move_z(name, v):
    with jax.named_scope(name):
        return lax.ppermute(v, ("z", "c"), pairs_zc(1))


def move_y(name, v):
    with jax.named_scope(name):
        return lax.ppermute(v, ("y", "c"), pairs_yc(1))


def move_x(name, v, d=1):
    with jax.named_scope(name):
        return lax.ppermute(v, ("c", "x"), pairs_cx(d))


def swap(name, v):
    with jax.named_scope(name):
        return lax.ppermute(v, "c", [(0, 1), (1, 0)])


def cost(flops, moved):
    return pl.CostEstimate(flops=flops, bytes_accessed=moved, transcendentals=0)


def in_smem():
    return pl.BlockSpec(memory_space=pltpu.SMEM)


def in_vmem():
    return pl.BlockSpec(memory_space=pltpu.VMEM)


def prepare_kernel(t_mask_ref, v_mask_ref, t_hbm, v_ref, t_out, v_out, perm, t_ref, sem):
    rows, cols = t_ref.shape
    fetch = pltpu.make_async_copy(t_hbm, t_ref, sem)
    fetch.start()
    z, y, c = (lax.axis_index(n) for n in ("z", "y", "c"))
    s = 1 - 2 * c
    for g in range(8):
        for k in range(CHUNK // 16):
            row = g * CHUNK + k * 16
            v = v_ref[row : row + 16, :]
            v = jnp.where(v_mask_ref[0, row // TILE] != 0, v, jnp.zeros_like(v))
            for zz in range(2):
                for yy in range(2):
                    v_out[(zz * 4 + g // 2) * NY + yy * 2 + g % 2, k * 16 : k * 16 + 16, :] = v

    source = lax.broadcasted_iota(jnp.int32, (cols, cols), 0)
    target = lax.broadcasted_iota(jnp.int32, (cols, cols), 1)
    shift = jnp.zeros((1, cols), jnp.int32)
    lane = lax.broadcasted_iota(jnp.int32, (1, cols), 1)
    steps = ((0, 0), (-s, 0), (s, 0), (0, 1), (2, 0), (-s, 1), (s, 1), (2, 1))
    for q, (dz, dy) in enumerate(steps):
        g = lax.rem(z + dz + NZ, 4) * 2 + lax.rem(y + dy, 2)
        shift = jnp.where(lane >= q * CHUNK, (g - q) * CHUNK, shift)
    perm[...] = jnp.where(source == target + shift, 1.0, 0.0).astype(perm.dtype)
    fetch.wait()

    @pl.loop(0, rows // ROWS)
    def _(i):
        start = pl.multiple_of(i * ROWS, ROWS)
        bands = []
        for a in range(ROWS // TILE):
            tiles = []
            for j in range(cols // TILE):
                t = t_ref[pl.ds(start + a * TILE, TILE), j * TILE : (j + 1) * TILE]
                tiles.append(jnp.where(t_mask_ref[j, i * (ROWS // TILE) + a] != 0, t, jnp.zeros_like(t)))
            bands.append(jnp.concatenate(tiles, axis=1))
        kept = jnp.concatenate(bands, axis=0)
        t_out[pl.ds(start, ROWS), :] = jnp.dot(kept, perm[...], preferred_element_type=jnp.float32).astype(t_out.dtype)


def prepare(t_mask, v_mask, t, v):
    return pl.pallas_call(
        prepare_kernel,
        out_shape=(
            jax.ShapeDtypeStruct(t.shape, t.dtype),
            jax.ShapeDtypeStruct((NZ * NY, CHUNK, TILE), v.dtype),
        ),
        in_specs=[in_smem()] * 2 + [pl.BlockSpec(memory_space=pl.ANY), in_vmem()],
        out_specs=(in_vmem(), in_vmem()),
        scratch_shapes=[pltpu.VMEM((t.shape[1], t.shape[1]), t.dtype), pltpu.VMEM(t.shape, t.dtype), pltpu.SemaphoreType.DMA],
        compiler_params=pltpu.CompilerParams(vmem_limit_bytes=WHOLE),
        cost_estimate=cost(2 * t.size * t.shape[1], 4 * t.size + 12 * v.size),
        name="prepare",
    )(t_mask.T, v_mask.T, t, v)


def select_kernel(pick_ref, a_ref, b_ref, own_ref, near_ref, far_ref):
    start = 0
    for out_ref in (own_ref, near_ref, far_ref):
        for j in range(out_ref.shape[0]):
            k = pick_ref[start + j]
            chip = lax.rem(k, NZ * NY)
            out_ref[j] = jnp.where(k < NZ * NY, a_ref[chip], b_ref[chip])
        start += out_ref.shape[0]


def select(picks, a, b):
    shape = lambda n: jax.ShapeDtypeStruct((n, CHUNK, TILE), a.dtype)
    return pl.pallas_call(
        select_kernel,
        out_shape=(shape(COLS), shape(COLS), shape(HALF)),
        in_specs=[in_smem(), in_vmem(), in_vmem()],
        out_specs=(in_vmem(),) * 3,
        compiler_params=pltpu.CompilerParams(vmem_limit_bytes=SMALL),
        cost_estimate=cost(0, 2 << 20),
        name="select_columns",
    )(picks, a, b)


def column_picks(order):
    c, x = lax.axis_index("c"), lax.axis_index("x")
    lane = jnp.arange(2 * COLS + HALF, dtype=jnp.int32)
    near = lax.rem(x + 1 - 2 * c + NX, NX) * COLS + lane - COLS
    far = lax.rem(x + 2, NX) * COLS + c * HALF + lane - 2 * COLS
    wanted = jnp.where(lane < COLS, x * COLS + lane, jnp.where(lane < 2 * COLS, near, far))
    stored = jnp.arange(order.shape[0], dtype=jnp.int32)
    held = stored // 2 + jnp.where(stored % 2 == c, 0, NZ * NY)
    return jnp.sum(jnp.where(order[None, :] == wanted[:, None], held[None, :], 0), axis=1).astype(jnp.int32)


def pack_kernel(own_ref, r1_ref, w1_ref, r2_ref, w2_ref, ahead_ref, rest_ref):
    c = lax.axis_index("c")
    for j in range(COLS):
        opposite = jnp.where(c == j // HALF, r2_ref[j % HALF], w2_ref[j % HALF])
        left = jnp.where(c == 0, r1_ref[j], w1_ref[j])
        right = jnp.where(c == 0, w1_ref[j], r1_ref[j])
        ahead_ref[j, 0] = jnp.where(c == 0, own_ref[j], left)
        ahead_ref[j, 1] = jnp.where(c == 0, opposite, right)
        rest_ref[j, 0] = jnp.where(c == 0, left, own_ref[j])
        rest_ref[j, 1] = jnp.where(c == 0, right, opposite)


def pack(own, r1, w1, r2, w2):
    shape = jax.ShapeDtypeStruct((COLS, 2, CHUNK, TILE), own.dtype)
    return pl.pallas_call(
        pack_kernel,
        out_shape=(shape, shape),
        in_specs=[in_vmem()] * 5,
        out_specs=(in_vmem(),) * 2,
        compiler_params=pltpu.CompilerParams(vmem_limit_bytes=SMALL),
        cost_estimate=cost(0, 3 << 20),
        name="pack_shard",
    )(own, r1, w1, r2, w2)


def arrange_kernel(t0, t1, t2, t3, early_ref, late_ref):
    c = lax.axis_index("c")
    rows, cols = t0.shape
    half = cols // 2

    def run(parts):
        @pl.loop(0, rows // TILE)
        def _(a):
            at = pl.ds(pl.multiple_of(a * TILE, TILE), TILE)
            whole = [p[at, :] for p in parts]
            early_ref[at, :] = jnp.concatenate([w[:, :half] for w in whole], axis=1)
            late_ref[at, :] = jnp.concatenate([w[:, half:] for w in whole], axis=1)

    @pl.when(c == 0)
    def _():
        run((t0, t3, t1, t2))

    @pl.when(c != 0)
    def _():
        run((t2, t1, t0, t3))


def arrange(ts):
    rows, cols = ts[0].shape
    shape = jax.ShapeDtypeStruct((rows, NX * cols // 2), ts[0].dtype)
    return pl.pallas_call(
        arrange_kernel,
        out_shape=(shape, shape),
        in_specs=[in_vmem()] * NX,
        out_specs=(in_vmem(), in_vmem()),
        compiler_params=pltpu.CompilerParams(vmem_limit_bytes=SMALL),
        cost_estimate=cost(0, 16 * rows * cols),
        name="arrange_t",
    )(*ts)


def product(t, blocks, n):
    columns = []
    for j in (n, n + 1):
        pieces = [blocks[q + r // 2 * 4][j, r % 2] for r in range(NX) for q in range(4)]
        columns.append(jnp.concatenate(pieces, axis=0))
    return jnp.dot(t, jnp.concatenate(columns, axis=1), preferred_element_type=jnp.float32)


def early_kernel(first, mask_ref, t_ref, r_ref, *rest):
    blocks, acc_ref = rest[:8], rest[8]

    @pl.loop(0, t_ref.shape[0] // ROWS)
    def _(i):
        at = pl.multiple_of(i * ROWS, ROWS)
        t = t_ref[pl.ds(at, ROWS), :]
        for n in range(0, HALF, 2):
            part = product(t, blocks, first + n)
            for a in range(ROWS // TILE):
                rows = pl.ds(pl.multiple_of(at + a * TILE, TILE), TILE)
                for j in range(2):
                    m = mask_ref[i * (ROWS // TILE) + a, first + n + j].astype(jnp.float32)
                    kept = part[a * TILE : (a + 1) * TILE, j * TILE : (j + 1) * TILE] * m
                    old = r_ref[rows, (first + n + j) * TILE : (first + n + j + 1) * TILE].astype(jnp.float32)
                    acc_ref[rows, (n + j) * TILE : (n + j + 1) * TILE] = old + kept


def early(first, r_mask, t, r_old, blocks):
    rows, depth = t.shape
    width = HALF * TILE
    return pl.pallas_call(
        functools.partial(early_kernel, first),
        out_shape=jax.ShapeDtypeStruct((rows, width), jnp.float32),
        in_specs=[in_smem()] + [in_vmem()] * 10,
        out_specs=in_vmem(),
        compiler_params=pltpu.CompilerParams(vmem_limit_bytes=LARGE),
        cost_estimate=cost(2 * rows * depth * width, 6 * rows * width + 2 * rows * depth + 2 * depth * width),
        name="ladder_early",
    )(r_mask, t, r_old, *blocks)


def late_kernel(mask_ref, t_ref, acc0, acc1, *rest):
    blocks, (out_ref, buffer, sems) = rest[:8], rest[8:]
    steps = t_ref.shape[0] // ROWS

    def send(i):
        rows = pl.ds(pl.multiple_of(i * ROWS, ROWS), ROWS)
        return pltpu.make_async_copy(buffer.at[i], out_ref.at[rows, :], sems.at[i])

    @pl.loop(0, steps)
    def _(i):
        at = pl.multiple_of(i * ROWS, ROWS)
        t = t_ref[pl.ds(at, ROWS), :]
        for n in range(0, COLS, 2):
            part = product(t, blocks, n)
            for a in range(ROWS // TILE):
                rows = pl.ds(pl.multiple_of(at + a * TILE, TILE), TILE)
                for j in range(2):
                    k = n + j
                    m = mask_ref[i * (ROWS // TILE) + a, k].astype(jnp.float32)
                    kept = part[a * TILE : (a + 1) * TILE, j * TILE : (j + 1) * TILE] * m
                    acc = (acc0, acc1)[k // HALF]
                    total = acc[rows, k % HALF * TILE : (k % HALF + 1) * TILE] + kept
                    buffer[i, a * TILE : (a + 1) * TILE, k * TILE : (k + 1) * TILE] = total.astype(buffer.dtype)
        send(i).start()

    @pl.loop(0, steps)
    def _(i):
        send(i).wait()


def late(r_mask, t, accs, blocks):
    rows, depth = t.shape
    width = COLS * TILE
    return pl.pallas_call(
        late_kernel,
        out_shape=jax.ShapeDtypeStruct((rows, width), t.dtype),
        in_specs=[in_smem()] + [in_vmem()] * 11,
        out_specs=pl.BlockSpec(memory_space=pl.ANY),
        scratch_shapes=[pltpu.VMEM((rows // ROWS, ROWS, width), t.dtype), pltpu.SemaphoreType.DMA((rows // ROWS,))],
        compiler_params=pltpu.CompilerParams(vmem_limit_bytes=LARGE),
        cost_estimate=cost(2 * rows * depth * width, 6 * rows * width + 2 * rows * depth + 2 * depth * width),
        name="ladder_late",
    )(r_mask, t, *accs, *blocks)


def body(t_amp, t_mask, v_int, v_mask, ab_order, r_mask, r_old):
    hold = lax.optimization_barrier
    picks = column_picks(ab_order)
    t0, spread = prepare(t_mask, v_mask, t_amp, v_int)
    t1 = move_x("t_near", t0)
    t2 = move_x("t_back", t0, -1)
    mine = lax.all_to_all(spread, ("z", "y"), 0, 0)
    partner = swap("v_swap", mine)
    own, near, opposite = select(picks, mine, partner)

    r1 = move_x("r_near", near)
    with jax.named_scope("r_far"):
        r2 = lax.ppermute(opposite, "x", [(i, (i + 2) % NX) for i in range(NX)])
    t1, t2, r1 = hold((t1, t2, r1))
    t3 = move_x("t_far", t1)
    w1, w2 = swap("r_near_swap", r1), swap("r_far_swap", r2)
    ahead, rest = pack(own, r1, w1, r2, w2)

    p1a = move_z("p1a", ahead)
    p1r = move_z("p1r", rest)
    q0 = move_y("q0", ahead)
    p2, q1a, q1r = move_z("p2", p1a), move_z("q1a", q0), move_y("q1r", p1r)
    q2 = move_y("q2", p2)
    t_early, t_late = arrange((t0, t1, t2, t3))
    p1a_swap, near_r, t_early = hold((swap("p1a_swap", p1a), p1r, t_early))
    p1r_swap = swap("p1r_swap", near_r)
    blocks = (ahead, p1a, p1r_swap, q0, rest, p1r, p1a_swap, swap("q0_swap", q0))
    acc0 = early(0, r_mask, t_early, r_old, blocks)
    p2h, acc0 = hold((p2, acc0))
    acc1 = early(HALF, r_mask, t_early, r_old, blocks)
    q1a, q1r, acc1 = hold((q1a, q1r, acc1))
    q1a_swap, q1r_swap, p2_swap = swap("q1a_swap", q1a), swap("q1r_swap", q1r), swap("p2_swap", p2h)
    q2, q1a_swap, q1r_swap, p2_swap = hold((q2, q1a_swap, q1r_swap, p2_swap))
    accs = (acc0, acc1)
    blocks = (p2h, q1a, q1r_swap, q2, p2_swap, q1r, q1a_swap, swap("q2_swap", q2))
    return late(r_mask, t_late, accs, blocks)


def solution(mesh):
    torus = Mesh(mesh.devices.reshape(NZ, NY, 2, NX), ("z", "y", "c", "x"))
    pair = ("z", "y", "c")
    placed = (P(pair, "x"), P(pair, "x"), P("x", pair), P("x", pair), P(), P(pair, "x"), P(pair, "x"))
    return jax.shard_map(body, mesh=torus, in_specs=placed, out_specs=P(pair, "x"), check_vma=False)
```
